32 devices in a mesh: groups: 2 (over y), dp: 4 (over x, core), tensor: 4 (over z).
Axes of the slice: x: 2, y: 2, z: 4, core: 2. Of those that a mesh axis runs over, the one named last changes fastest.
Arguments:
- gate_pre: bfloat16 [2048, 16384], P(('groups', 'dp'), 'tensor'), parts along dimension 0, may hold values from -6 to 6
- up_pre: bfloat16 [2048, 16384], P(('groups', 'dp'), 'tensor'), parts along dimension 0, may hold values from -6 to 6
- down_weight: bfloat16 [16384, 4096], P('tensor', 'dp'), may hold values from -0.0625 to 0.0625
- block_mask: int32 [128, 32], P('tensor'), may hold values from 0 to 1, as said below
- grad_out: bfloat16 [2048, 4096], P(('groups', 'dp'), 'tensor'), parts along dimension 0, may hold values from -6 to 6
Outputs:
- output: bfloat16 [2048, 4096], P(('groups', 'dp'), 'tensor'), parts along dimension 0
- d_gate: bfloat16 [2048, 16384], P(('groups', 'dp'), 'tensor'), parts along dimension 0
- d_up: bfloat16 [2048, 16384], P(('groups', 'dp'), 'tensor'), parts along dimension 0
- d_weight: float32 [32768, 4096], P(('groups', 'tensor'), 'dp'), parts along dimension 0
The draws below stay inside these ranges and needn't reach their ends.
There are 2 independent parts, one for each index of `groups`. The reference program is written for one: setup_inputs(seed, part) draws one part's arguments, and reference() takes and returns one part's arrays. A program takes and returns all parts, laid end to end along the dimension named above; an argument that names none is the same for every part. Nothing has to cross between parts.
Inputs may be any that keep to these rules, and one draw needn't show every extreme that they name: block_mask holds 0 and 1. In each device's shard of down_weight (32 block rows of one tensor index by 8 block columns of one dp index) between 96 and 160 blocks are kept; all shards of some tensor index keep exactly 160.
All inputs are finite; a program needn't handle non-finite values.
Results may differ from the reference program's by a relative error of at most 0.0051.
Values may be sent and summed in bfloat16 or wider, within the bound.
No kernel may reach another device: no remote copies, remote signals or barrier semaphores. Data moves between devices by JAX's collectives and lax.ppermute only.
A program may use at most 192 MiB of HBM per device.

```python
import jax
import jax.numpy as jnp

D = 4096
FF = 16384
BLK = 128
TOKENS = 1024
FBLK = 128
DBLK = 32
FB_DEV = 32
DB_DEV = 8
SLAB = 256
KEEP_MOST = 160
KEEP_LEAST = 96


def draw_block_mask(key, part):
    key = jax.random.fold_in(key, 11)
    key_level, key_jitter, key_full, key_order = jax.random.split(key, 4)
    slab_rows = FBLK // FB_DEV
    slab_cols = DBLK // DB_DEV
    level_row = jax.random.randint(key_level, (slab_rows, 1), KEEP_LEAST, KEEP_MOST + 1)
    jitter = jax.random.randint(key_jitter, (slab_rows, slab_cols), 0, 2)
    counts = jnp.minimum(level_row + jitter, KEEP_MOST)
    full_row = jax.random.randint(key_full, (), 0, slab_rows)
    counts = jnp.where(jnp.arange(slab_rows)[:, None] == full_row, KEEP_MOST, counts)
    priority = jax.random.randint(key_order, (slab_rows, slab_cols, SLAB), 0, 65536) * SLAB + jnp.arange(SLAB, dtype=jnp.int32)
    placing = jnp.argsort(jnp.argsort(priority, axis=-1), axis=-1)
    kept_mask = (placing < counts[:, :, None]).astype(jnp.int32)
    kept_mask = kept_mask.reshape(slab_rows, slab_cols, FB_DEV, DB_DEV).transpose(0, 2, 1, 3)
    return kept_mask.reshape(FBLK, DBLK)


def raised(values, own_key, source, target, blocks, factor):
    def block_of(position):
        return (jnp.arange(values.shape[position]) // (values.shape[position] // blocks)).reshape((-1,) + (1,) * (values.ndim - 1 - position))

    one_side = jax.random.permutation(own_key, blocks)[block_of(target)]
    second = (block_of(target) + blocks // 2) % blocks
    return jnp.where((block_of(source) == one_side) | (block_of(source) == second), factor * values, values)


def block_scale(stream_key, dims, pieces, least, largest):
    def one(axis_at, shards_of):
        heights = jax.random.uniform(jax.random.fold_in(jax.random.fold_in(stream_key, 6), axis_at), (shards_of,), jnp.float32, least / len(pieces), largest / len(pieces))
        return jnp.repeat(jnp.exp(heights), dims[axis_at] // shards_of).reshape((-1,) + (1,) * (len(dims) - axis_at - 1))

    level = one(*pieces[0])
    for cut in pieces[1:]:
        level = level * one(*cut)
    return level


def centred(key, extent, scale, limit, pieces=(), kind=jnp.bfloat16):
    array = jax.random.normal(key, extent, jnp.float32) * scale
    if len(pieces) > 0:
        array = block_scale(key, extent, pieces, -0.22, 0.18) * array
    return jnp.clip(array, min=-limit, max=limit).astype(kind)


def bell_draw_with(key, shape, width, most, pieces, heavy, kind=jnp.bfloat16):
    result = width * jax.random.normal(key, shape, jnp.float32)
    if pieces:
        result = result * block_scale(key, shape, pieces, -0.22, 0.18)
    return jnp.clip(raised(result, jax.random.fold_in(key, 3), *heavy), -most, most).astype(kind)


def setup_inputs(seed: int = 0, part: int = 0) -> dict:
    key_of = jax.random.split(jax.random.key(seed), 6)
    own_keys = jax.random.split(jax.random.fold_in(key_of[5], part), 6)
    gate_pre = centred(own_keys[0], (TOKENS, FF), 1.0, 6.0, ((0, 4), (1, 4)))
    up_pre = centred(own_keys[1], (TOKENS, FF), 1.0, 6.0, ((0, 4), (1, 4)))
    down_weight = bell_draw_with(key_of[2], (FF, D), FF ** -0.5, 0.0625, ((0, 4), (1, 4)), (0, 1, 4, 2.0))
    block_mask = draw_block_mask(jax.random.fold_in(key_of[5], 71), part)
    grad_out = centred(own_keys[4], (TOKENS, D), 1.0, 6.0, ((0, 4), (1, 4)))
    return dict(gate_pre=gate_pre, up_pre=up_pre, down_weight=down_weight, block_mask=block_mask, grad_out=grad_out)


def expand_mask(small_mask):
    widened = jnp.repeat(jnp.repeat(small_mask, BLK, axis=0), BLK, axis=1)
    return widened


def reference(gate_pre, up_pre, down_weight, block_mask, grad_out):
    keep_wide = expand_mask(block_mask)
    masked = down_weight * keep_wide.astype(jnp.bfloat16)
    gate_val = gate_pre.astype(jnp.float32)
    up_val = up_pre.astype(jnp.float32)
    gate_sig = jax.nn.sigmoid(gate_val)
    active = gate_val * gate_sig
    hidden = (active * up_val).astype(jnp.bfloat16)
    output = jnp.dot(hidden, masked, preferred_element_type=jnp.float32).astype(jnp.bfloat16)
    d_hidden = jnp.dot(grad_out, masked.T, preferred_element_type=jnp.float32)
    d_gate = (d_hidden * up_val * gate_sig * (1.0 + gate_val * (1.0 - gate_sig))).astype(jnp.bfloat16)
    d_up = (d_hidden * active).astype(jnp.bfloat16)
    d_weight = jnp.dot(hidden.T, grad_out, preferred_element_type=jnp.float32) * keep_wide.astype(jnp.float32)
    return (output, d_gate, d_up, d_weight)
```

```python
import functools

import jax
import jax.numpy as jnp
from jax import lax
from jax.experimental import pallas as pl
from jax.experimental.pallas import tpu as pltpu
from jax.sharding import PartitionSpec as P

BLK = 128
BF = jnp.bfloat16
F32 = jnp.float32
ROWS_CONTRACT = (((0,), (0,)), ((), ()))
COLS_CONTRACT = (((1,), (1,)), ((), ()))


def expand_mask(small_mask):
    widened = jnp.repeat(jnp.repeat(small_mask, BLK, axis=0), BLK, axis=1)
    return widened


def any_mesh(gate_pre, up_pre, down_weight, block_mask, grad_out):
    d_local = down_weight.shape[1]
    d_blocks = d_local // BLK
    own_mask = lax.dynamic_slice_in_dim(block_mask, lax.axis_index("dp") * d_blocks, d_blocks, 1)
    keep_wide = expand_mask(own_mask)
    masked = down_weight * keep_wide.astype(BF)
    gate_val = gate_pre.astype(F32)
    up_val = up_pre.astype(F32)
    gate_sig = jax.nn.sigmoid(gate_val)
    active = gate_val * gate_sig
    hidden = (active * up_val).astype(BF)
    full_grad = lax.all_gather(grad_out, "tensor", axis=1, tiled=True)
    gathered = lax.all_gather(masked, "dp", axis=1, tiled=True)
    d_hidden = lax.dot_general(full_grad, gathered, COLS_CONTRACT, preferred_element_type=F32)
    output = lax.psum_scatter(
        jnp.dot(hidden, gathered, preferred_element_type=F32),
        "tensor",
        scatter_dimension=1,
        tiled=True,
    ).astype(BF)
    d_gate = (d_hidden * up_val * gate_sig * (1.0 + gate_val * (1.0 - gate_sig))).astype(BF)
    d_up = (d_hidden * active).astype(BF)
    grad_cols = lax.all_to_all(full_grad, "dp", split_axis=1, concat_axis=0, tiled=True)
    d_weight = lax.dot_general(
        lax.all_gather(hidden, "dp", axis=0, tiled=True),
        grad_cols,
        ROWS_CONTRACT,
        preferred_element_type=F32,
    )
    d_weight = d_weight * keep_wide.astype(F32)
    return (output, d_gate, d_up, d_weight)


def mask_body(info, own, other, out):
    i = pl.program_id(0)
    half = own.shape[1]
    blocks = half // BLK
    row_blocks = own.shape[0] // BLK
    own_is_near = info[info.shape[0] - 1, 0]

    def put(src, first):
        for r in range(row_blocks):
            for k in range(blocks):
                keep = info[i * row_blocks + r, first + k].astype(F32)
                block = src[r * BLK : (r + 1) * BLK, k * BLK : (k + 1) * BLK]
                col = (first + k) * BLK
                out[r * BLK : (r + 1) * BLK, col : col + BLK] = (block.astype(F32) * keep).astype(BF)

    @pl.when(own_is_near == 1)
    def _():
        put(own, 0)
        put(other, blocks)

    @pl.when(own_is_near == 0)
    def _():
        put(other, 0)
        put(own, blocks)


def masked_pair(info, own, other):
    rows, half = own.shape
    step = 256
    return pl.pallas_call(
        mask_body,
        out_shape=jax.ShapeDtypeStruct((rows, 2 * half), BF),
        grid_spec=pltpu.PrefetchScalarGridSpec(
            num_scalar_prefetch=1,
            grid=(rows // step,),
            in_specs=[
                pl.BlockSpec((step, half), lambda i, _: (i, 0)),
                pl.BlockSpec((step, half), lambda i, _: (i, 0)),
            ],
            out_specs=pl.BlockSpec((step, 2 * half), lambda i, _: (i, 0)),
        ),
        compiler_params=pltpu.CompilerParams(vmem_limit_bytes=32 * 2**20),
        name="masked_pair",
    )(info, own, other)


def dw_body(n, keep_ref, *refs):
    hid, grads, out = refs[:n], refs[n : 2 * n], refs[2 * n]
    i = pl.program_id(0)
    total = None
    for h, g in zip(hid, grads):
        part = lax.dot_general(h[...], g[...], ROWS_CONTRACT, preferred_element_type=F32)
        total = part if total is None else total + part
    for r in range(out.shape[0] // BLK):
        for k in range(out.shape[1] // BLK):
            keep = keep_ref[i * (out.shape[0] // BLK) + r, k].astype(F32)
            rows, cols = slice(r * BLK, (r + 1) * BLK), slice(k * BLK, (k + 1) * BLK)
            out[rows, cols] = total[rows, cols] * keep


def weight_grad(keep, hidden, grads):
    n = len(hidden)
    hid_all = hidden[0].shape[1]
    cols = grads[0].shape[1]
    step = 512
    return pl.pallas_call(
        functools.partial(dw_body, n),
        out_shape=jax.ShapeDtypeStruct((hid_all, cols), F32),
        grid_spec=pltpu.PrefetchScalarGridSpec(
            num_scalar_prefetch=1,
            grid=(hid_all // step,),
            in_specs=[pl.BlockSpec((h.shape[0], step), lambda i, _: (0, i)) for h in hidden]
            + [pl.BlockSpec(g.shape, lambda i, _: (0, 0)) for g in grads],
            out_specs=pl.BlockSpec((step, cols), lambda i, _: (i, 0)),
        ),
        compiler_params=pltpu.CompilerParams(vmem_limit_bytes=48 * 2**20),
        name="weight_grad",
    )(keep, *hidden, *grads)


def four_by_four(gate_pre, up_pre, down_weight, block_mask, grad_out):
    n_dp = n_t = 4
    d, z = lax.axis_index("dp"), lax.axis_index("tensor")
    x, c = d // 2, d % 2
    q = jnp.where(x == 0, z, n_t - 1 - z)
    near = 2 * x + (1 - x)
    far = 2 * x + x
    own_near = d == near
    tokens, hid = gate_pre.shape
    cols = down_weight.shape[1]
    d_blocks = cols // BLK

    def place(dd, qq):
        return dd * n_t + (qq if dd // 2 == 0 else n_t - 1 - qq)

    def hop(a, *pairs):
        perm = [(place(dd, s), place(dd, t)) for dd in range(n_dp) for s, t in pairs]
        return lax.ppermute(a, ("dp", "tensor"), perm)

    def over_x(a):
        return lax.ppermute(a, "dp", [(i, i ^ 2) for i in range(n_dp)])

    def over_core(a):
        return lax.ppermute(a, "dp", [(i, i ^ 1) for i in range(n_dp)])

    roots = [(dd, qq) for dd in range(n_dp) for qq in (0, 1)]

    def to_roots(a):
        perm = [((dd ^ 2) * n_t + place(dd, qq) % n_t, place(dd, qq)) for dd, qq in roots]
        return lax.ppermute(a, ("dp", "tensor"), perm)

    def from_roots(a):
        perm = [(place(dd, qq), (dd ^ 2) * n_t + place(dd, qq) % n_t) for dd, qq in roots]
        return lax.ppermute(a, ("dp", "tensor"), perm)

    def pass_along(g):
        r1 = hop(g, (0, 1), (1, 2))
        dn = hop(g, (1, 0))
        r2 = hop(r1, (1, 2), (2, 3))
        r3 = hop(r2, (2, 3))
        g_near = jnp.where(q == 0, dn, jnp.where(q == 1, g, jnp.where(q == 2, r1, r2)))
        g_far = jnp.where(q == 0, g, jnp.where(q == 1, r1, jnp.where(q == 2, r2, r3)))
        return g_near, g_far

    grad_x = to_roots(grad_out)
    near1, far1 = pass_along(grad_x)
    near0, far0 = pass_along(grad_out)

    gate_val = gate_pre.astype(F32)
    up_val = up_pre.astype(F32)
    gate_sig = jax.nn.sigmoid(gate_val)
    active = gate_val * gate_sig
    hidden0 = (active * up_val).astype(BF)
    half = tokens // 2
    hidden1 = [over_x(hidden0[i * half : (i + 1) * half]) for i in range(2)]

    other = over_core(down_weight)
    keep_near = lax.dynamic_slice_in_dim(block_mask, near * d_blocks, d_blocks, 1)
    keep_far = lax.dynamic_slice_in_dim(block_mask, far * d_blocks, d_blocks, 1)
    keep_own = lax.dynamic_slice_in_dim(block_mask, d * d_blocks, d_blocks, 1)
    flag = jnp.full((1, 2 * d_blocks), own_near, jnp.int32)
    info = jnp.concatenate([jnp.concatenate([keep_near, keep_far], 1), flag], 0)
    pair = masked_pair(info, down_weight, other)

    def reduced(h):
        o = jnp.dot(h, pair, preferred_element_type=F32)
        o_near, o_far = o[:, :cols], o[:, cols:]
        e1 = hop(o_far.astype(BF), (3, 2))
        e2 = hop(o_near.astype(BF), (3, 2), (0, 1))
        e3 = hop((o_far + e1.astype(F32)).astype(BF), (2, 1))
        o_near = o_near + e2.astype(F32)
        e4 = hop(o_near.astype(BF), (2, 1))
        e5 = hop((o_far + e3.astype(F32)).astype(BF), (1, 0))
        return jnp.where(q == 0, o_far + e5.astype(F32), o_near + e4.astype(F32)).astype(BF)

    out1 = [from_roots(reduced(h)) for h in hidden1]
    out0 = reduced(hidden0)
    output = jnp.where(q < 2, out0, jnp.concatenate(out1, 0))

    both1 = jnp.concatenate([near1, far1], 1)
    both0 = jnp.concatenate([near0, far0], 1)
    n_chunk = 4
    width = hid // n_chunk
    d_gate, d_up = [], []
    for k in range(n_chunk):
        s = slice(k * width, (k + 1) * width)
        w = pair[s]
        sent = lax.dot_general(both1, w, COLS_CONTRACT, preferred_element_type=F32).astype(BF)
        got = over_x(sent)
        d_hidden = lax.dot_general(both0, w, COLS_CONTRACT, preferred_element_type=F32)
        d_hidden = d_hidden + got.astype(F32)
        gv, uv, sg = gate_val[:, s], up_val[:, s], gate_sig[:, s]
        d_gate.append((d_hidden * uv * sg * (1.0 + gv * (1.0 - sg))).astype(BF))
        d_up.append((d_hidden * active[:, s]).astype(BF))
    d_gate = jnp.concatenate(d_gate, 1)
    d_up = jnp.concatenate(d_up, 1)

    hidden1_all = jnp.concatenate(hidden1, 0)
    hidden2 = over_core(hidden0)
    hidden3 = over_core(hidden1_all)
    mine = [jnp.where(own_near, a, b) for a, b in ((near0, far0), (near1, far1))]
    theirs = [over_core(jnp.where(own_near, b, a)) for a, b in ((near0, far0), (near1, far1))]
    d_weight = weight_grad(keep_own, [hidden0, hidden1_all, hidden2, hidden3], mine + theirs)
    return (output, d_gate, d_up, d_weight)


def solution(mesh):
    fits = mesh.shape["dp"] == 4 and mesh.shape["tensor"] == 4
    return jax.shard_map(
        four_by_four if fits else any_mesh,
        mesh=mesh,
        in_specs=(
            P(("groups", "dp"), "tensor"),
            P(("groups", "dp"), "tensor"),
            P("tensor", "dp"),
            P("tensor", None),
            P(("groups", "dp"), "tensor"),
        ),
        out_specs=(
            P(("groups", "dp"), "tensor"),
            P(("groups", "dp"), "tensor"),
            P(("groups", "dp"), "tensor"),
            P(("groups", "tensor"), "dp"),
        ),
        check_vma=False,
    )
```

```python
import math

import jax
import jax.numpy as jnp
from jax import lax
from jax.experimental import pallas as pl
from jax.experimental.pallas import tpu as pltpu
from jax.sharding import PartitionSpec as P

BLK = 128
BF = jnp.bfloat16
F32 = jnp.float32
ROWS_CONTRACT = (((0,), (0,)), ((), ()))
COLS_CONTRACT = (((1,), (1,)), ((), ()))


def expand_mask(small_mask):
    widened = jnp.repeat(jnp.repeat(small_mask, BLK, axis=0), BLK, axis=1)
    return widened


def any_mesh(gate_pre, up_pre, down_weight, block_mask, grad_out):
    d_local = down_weight.shape[1]
    d_blocks = d_local // BLK
    own_mask = lax.dynamic_slice_in_dim(block_mask, lax.axis_index("dp") * d_blocks, d_blocks, 1)
    keep_wide = expand_mask(own_mask)
    masked = down_weight * keep_wide.astype(BF)
    gate_val = gate_pre.astype(F32)
    up_val = up_pre.astype(F32)
    gate_sig = jax.nn.sigmoid(gate_val)
    active = gate_val * gate_sig
    hidden = (active * up_val).astype(BF)
    full_grad = lax.all_gather(grad_out, "tensor", axis=1, tiled=True)
    gathered = lax.all_gather(masked, "dp", axis=1, tiled=True)
    d_hidden = lax.dot_general(full_grad, gathered, COLS_CONTRACT, preferred_element_type=F32)
    output = lax.psum_scatter(
        jnp.dot(hidden, gathered, preferred_element_type=F32),
        "tensor",
        scatter_dimension=1,
        tiled=True,
    ).astype(BF)
    d_gate = (d_hidden * up_val * gate_sig * (1.0 + gate_val * (1.0 - gate_sig))).astype(BF)
    d_up = (d_hidden * active).astype(BF)
    grad_cols = lax.all_to_all(full_grad, "dp", split_axis=1, concat_axis=0, tiled=True)
    d_weight = lax.dot_general(
        lax.all_gather(hidden, "dp", axis=0, tiled=True),
        grad_cols,
        ROWS_CONTRACT,
        preferred_element_type=F32,
    )
    d_weight = d_weight * keep_wide.astype(F32)
    return (output, d_gate, d_up, d_weight)


IN_VMEM = pl.BlockSpec(memory_space=pltpu.VMEM)
IN_SMEM = pl.BlockSpec(memory_space=pltpu.SMEM)
ANYWHERE = pl.BlockSpec(memory_space=pl.ANY)


LARGE = 1536 * 1024


def shaped(shape, dtype):
    size = math.prod(shape) * jnp.dtype(dtype).itemsize
    return (pltpu.HBM if size >= LARGE else jax.ShapeDtypeStruct)(shape, dtype)


def placed(a):
    return pltpu.with_memory_space_constraint(a, pltpu.HBM) if a.size * a.dtype.itemsize >= LARGE else a


def ordered(body, deps, operands, out_shape, *, name, pair=None, flops=1, in_specs=None, out_specs=None, grid=(), scratch=(), aliases=None):
    n, m = len(operands), len(deps)
    one = not isinstance(out_shape, (list, tuple))
    operands = [a if a is pair else placed(a) for a in operands]
    deps = [placed(a) for a in deps]

    def run(*refs):
        body(*refs[:n], *refs[n + m :])

    in_specs = [IN_VMEM] * n if in_specs is None else list(in_specs)
    if out_specs is None:
        out_specs = IN_VMEM if one else [IN_VMEM] * len(out_shape)
    return pl.pallas_call(
        run,
        grid=grid,
        in_specs=in_specs + [ANYWHERE] * m,
        out_specs=out_specs,
        out_shape=out_shape,
        scratch_shapes=scratch,
        input_output_aliases=aliases or {},
        compiler_params=pltpu.CompilerParams(vmem_limit_bytes=18 * 2**20),
        cost_estimate=pl.CostEstimate(flops=flops, bytes_accessed=1, transcendentals=0),
        name=name,
    )(*operands, *deps)


def kept(w, mask_ref, row, first, rep):
    n, cols = w.shape[0] // BLK, w.shape[1]
    out = []
    for r in range(n):
        keep = [jnp.full((rep, BLK), mask_ref[row + r, first + k].astype(F32)) for k in range(cols // BLK)]
        m = jnp.concatenate(keep, 1).astype(w.dtype).reshape(1, rep, cols)
        rows = w[r * BLK : (r + 1) * BLK, :].reshape(BLK // rep, rep, cols) * m
        out.append(rows.reshape(BLK, cols))
    return jnp.concatenate(out, 0)


def hidden_of(gate, up, deps):
    rows, hid = gate.shape
    unit = 64

    def body(gate_ref, up_ref, out):
        g = gate_ref[...].astype(F32)
        out[...] = (g * jax.nn.sigmoid(g) * up_ref[...].astype(F32)).astype(BF)

    at = pl.BlockSpec((unit, hid), lambda i: (i, 0))
    return ordered(
        body,
        deps,
        [gate, up],
        shaped((rows, hid), BF),
        grid=(rows // unit,),
        in_specs=[at, at],
        out_specs=at,
        name="hidden",
    )


def masked_pair(info, mask, own, other, deps):
    hid, cols = own.shape
    step = 512

    def body(info_ref, mask_ref, a, b, out):
        row = pl.program_id(0) * (step // BLK)
        x, core = info_ref[0], info_ref[1]
        out[core] = kept(a[...], mask_ref, row, (2 * x + core) * (cols // BLK), 16)
        out[1 - core] = kept(b[...], mask_ref, row, (2 * x + 1 - core) * (cols // BLK), 16)

    w = pl.BlockSpec((step, cols), lambda k: (k, 0))
    pair = ordered(
        body,
        deps,
        [info, mask, own, other],
        pltpu.VMEM((2, hid, cols), BF),
        grid=(hid // step,),
        in_specs=[IN_SMEM, IN_SMEM, w, w],
        out_specs=pl.BlockSpec((2, step, cols), lambda k: (0, k, 0)),
        name="masked_pair",
    )
    return pltpu.with_memory_space_constraint(pair, pltpu.VMEM)


def forward_own(hidden, pair, deps):
    rows, cols = hidden.shape[0], pair.shape[2]

    def body(h, w, out):
        for j in range(2):
            out[j] = jnp.dot(h[...], w[j], preferred_element_type=F32).astype(BF)

    return ordered(body, deps, [hidden, pair], shaped((2, rows, cols), BF), name="forward_own", pair=pair)


def forward_both(info, own, hidden, pair, deps):
    rows, cols = hidden.shape[0], pair.shape[2]

    def body(info_ref, o, h, w, out):
        x = info_ref[0]
        for j in range(2):
            part = jnp.dot(h[...], w[j], preferred_element_type=F32).astype(BF)
            out[jnp.where(x == 0, 3 - 2 * j, 2 - 2 * j)] = part
            out[jnp.where(x == 0, 2 * j, 1 + 2 * j)] = o[j]

    return ordered(
        body,
        deps,
        [info, own, hidden, pair],
        shaped((4, rows, cols), BF),
        in_specs=[IN_SMEM] + [IN_VMEM] * 3,
        name="forward_both",
        pair=pair,
    )


def cut(info, grads, deps):
    rows, cols = grads.shape
    half = cols // 2

    def body(info_ref, g, mine, theirs):
        x = info_ref[0]
        mine[...] = g[:, pl.ds(pl.multiple_of(x * half, half), half)]
        theirs[...] = g[:, pl.ds(pl.multiple_of((1 - x) * half, half), half)]

    out = jax.ShapeDtypeStruct((rows, half), BF)
    return ordered(body, deps, [info, grads], [out, out], in_specs=[IN_SMEM, IN_VMEM], name="cut")


def per_core(info, g0, g1, deps):
    rows, cols = g0.shape
    half = cols // 2

    def body(info_ref, a, b, mine, theirs):
        core = info_ref[1]
        for at, g in enumerate((a, b)):
            s = slice(at * rows, (at + 1) * rows)
            mine[s, :] = g[:, pl.ds(pl.multiple_of(core * half, half), half)]
            theirs[s, :] = g[:, pl.ds(pl.multiple_of((1 - core) * half, half), half)]

    out = jax.ShapeDtypeStruct((2 * rows, half), BF)
    return ordered(body, deps, [info, g0, g1], [out, out], in_specs=[IN_SMEM, IN_VMEM, IN_VMEM], name="per_core")


def back(grads, pair, first, width, dtype, deps, flops=1):
    step = 512
    cols = pair.shape[2]

    def body(g, w, out):
        for k in range(0, width, step):
            rows = slice(first + k, first + k + step)
            part = lax.dot_general(g[:, :cols], w[0, rows, :], COLS_CONTRACT, preferred_element_type=F32)
            part += lax.dot_general(g[:, cols:], w[1, rows, :], COLS_CONTRACT, preferred_element_type=F32)
            out[:, k : k + step] = part.astype(dtype)

    return ordered(body, deps, [grads, pair], shaped((grads.shape[0], width), dtype), name="back", pair=pair, flops=flops)


def relay(a, deps):
    def body(src, out):
        out[...] = src[...]

    return ordered(body, deps, [a], shaped(a.shape, a.dtype), name="relay")


def choose(info, own, received, deps):
    def body(info_ref, a, b, out):
        out[...] = jnp.where(info_ref[2] == 0, a[...], b[...])

    return ordered(
        body, deps, [info, own, received], shaped(own.shape, BF), in_specs=[IN_SMEM, IN_VMEM, IN_VMEM], name="choose"
    )


def hidden_grads(part, got, gate, up, first, made, deps):
    rows, width = got.shape
    unit = 512

    def body(p, r, gate_ref, up_ref, *refs):
        d_gate, d_up = refs[-2:]
        g, u = gate_ref[...].astype(F32), up_ref[...].astype(F32)
        s = jax.nn.sigmoid(g)
        d_hidden = p[...] + r[...].astype(F32)
        d_gate[...] = (d_hidden * u * s * (1.0 + g * (1.0 - s))).astype(BF)
        d_up[...] = (d_hidden * (g * s)).astype(BF)

    at = pl.BlockSpec((rows, unit), lambda k: (0, first // unit + k))
    return ordered(
        body,
        deps,
        [part, got, gate, up, *made],
        [shaped(gate.shape, BF)] * 2,
        grid=(width // unit,),
        in_specs=[at, pl.BlockSpec((rows, unit), lambda k: (0, k)), at, at] + [ANYWHERE] * len(made),
        out_specs=[at, at],
        aliases={4: 0, 5: 1} if made else None,
        name="hidden_grads",
    )


def weight_grad(info, mask, hidden, grads, deps):
    n = len(hidden)
    rows = sum(h.shape[0] for h in hidden)
    hid, cols = hidden[0].shape[1], grads[0].shape[1]
    step = 512

    def body(info_ref, mask_ref, *refs):
        hid_refs, grad_refs, (out, all_grads) = refs[:n], refs[n:-2], refs[-2:]

        @pl.when(pl.program_id(0) == 0)
        def _():
            at = 0
            for g in grad_refs:
                all_grads[at : at + g.shape[0], :] = g[...]
                at += g.shape[0]

        h = jnp.concatenate([r[...] for r in hid_refs], 0)
        total = lax.dot_general(h, all_grads[...], ROWS_CONTRACT, preferred_element_type=F32)
        row = pl.program_id(0) * (step // BLK)
        out[...] = kept(total, mask_ref, row, (2 * info_ref[0] + info_ref[1]) * (cols // BLK), 8)

    return ordered(
        body,
        deps,
        [info, mask, *hidden, *grads],
        shaped((hid, cols), F32),
        grid=(hid // step,),
        in_specs=[IN_SMEM, IN_SMEM]
        + [pl.BlockSpec((h.shape[0], step), lambda i: (0, i)) for h in hidden]
        + [pl.BlockSpec(g.shape, lambda i: (0, 0)) for g in grads],
        out_specs=pl.BlockSpec((step, cols), lambda i: (i, 0)),
        scratch=[pltpu.VMEM((rows, cols), BF)],
        name="weight_grad",
    )


def four_by_four(gate_pre, up_pre, down_weight, block_mask, grad_out):
    n_t = 4
    d, z = lax.axis_index("dp"), lax.axis_index("tensor")
    x, core = d // 2, d % 2
    q = jnp.where(x == 0, z, n_t - 1 - z)
    tokens, hid = gate_pre.shape
    info = jnp.stack([x, core, q]).astype(jnp.int32)

    def over_x(a):
        return lax.ppermute(a, "dp", [(i, i ^ 2) for i in range(4)])

    def over_core(a):
        return lax.ppermute(a, "dp", [(i, i ^ 1) for i in range(4)])

    def to_owner(a):
        perm = []
        for dd in range(4):
            line = [0, 1, 2, 3] if dd // 2 == 0 else [3, 2, 1, 0]
            perm.append((dd * n_t + line[1], (dd ^ 2) * n_t + line[1]))
            perm.append((dd * n_t + line[2], dd * n_t + line[1]))
            perm.append((dd * n_t + line[3], (dd ^ 2) * n_t + line[0]))
        return lax.ppermute(a, ("dp", "tensor"), perm)

    other = over_core(down_weight)
    full_grad = lax.all_gather(grad_out, "tensor", axis=1, tiled=True)
    h0 = hidden_of(gate_pre, up_pre, [])
    h1 = over_x(h0)
    h2 = over_core(h0)
    pair = masked_pair(info, block_mask, down_weight, other, [h0])
    o0 = forward_own(h0, pair, [h2])
    g0, gx = cut(info, full_grad, [o0])
    g1 = over_x(gx)
    o_all = forward_both(info, o0, h1, pair, [g0])
    out = lax.psum_scatter(o_all, "tensor", scatter_dimension=0, tiled=False)
    h3 = over_core(h1)
    part = back(g0, pair, 0, hid, F32, [o_all])
    parts = [(0, 3 * hid // 8), (3 * hid // 8, 3 * hid // 8), (3 * hid // 4, hid // 4)]
    last, got = part, []
    for first, width in parts:
        last = back(g1, pair, first, width, BF, [last], 6 * 10**10)
        got.append(over_x(last))
    g_own, g_theirs = per_core(info, g0, g1, [last])
    g_core = over_core(g_theirs)
    d_weight = weight_grad(info, block_mask, [h0, h1, h2, h3], [g_own, g_core], [])
    made, deps = [], [d_weight]
    for (first, _), g in zip(parts, got):
        made, deps = list(hidden_grads(part, g, gate_pre, up_pre, first, made, deps)), []
    done = relay(out, [d_weight])
    output = choose(info, done, to_owner(done), [made[0]])
    return (output, *made, d_weight)


def solution(mesh):
    fits = mesh.shape["dp"] == 4 and mesh.shape["tensor"] == 4
    return jax.shard_map(
        four_by_four if fits else any_mesh,
        mesh=mesh,
        in_specs=(
            P(("groups", "dp"), "tensor"),
            P(("groups", "dp"), "tensor"),
            P("tensor", "dp"),
            P("tensor", None),
            P(("groups", "dp"), "tensor"),
        ),
        out_specs=(
            P(("groups", "dp"), "tensor"),
            P(("groups", "dp"), "tensor"),
            P(("groups", "dp"), "tensor"),
            P(("groups", "tensor"), "dp"),
        ),
        check_vma=False,
    )
```

```python
import math

import jax
import jax.numpy as jnp
from jax import lax
from jax.experimental import pallas as pl
from jax.experimental.pallas import tpu as pltpu
from jax.sharding import PartitionSpec as P

BLK = 128
BF = jnp.bfloat16
F32 = jnp.float32
ROWS_CONTRACT = (((0,), (0,)), ((), ()))
COLS_CONTRACT = (((1,), (1,)), ((), ()))


def expand_mask(small_mask):
    widened = jnp.repeat(jnp.repeat(small_mask, BLK, axis=0), BLK, axis=1)
    return widened


def any_mesh(gate_pre, up_pre, down_weight, block_mask, grad_out):
    d_local = down_weight.shape[1]
    d_blocks = d_local // BLK
    own_mask = lax.dynamic_slice_in_dim(block_mask, lax.axis_index("dp") * d_blocks, d_blocks, 1)
    keep_wide = expand_mask(own_mask)
    masked = down_weight * keep_wide.astype(BF)
    gate_val = gate_pre.astype(F32)
    up_val = up_pre.astype(F32)
    gate_sig = jax.nn.sigmoid(gate_val)
    active = gate_val * gate_sig
    hidden = (active * up_val).astype(BF)
    full_grad = lax.all_gather(grad_out, "tensor", axis=1, tiled=True)
    gathered = lax.all_gather(masked, "dp", axis=1, tiled=True)
    d_hidden = lax.dot_general(full_grad, gathered, COLS_CONTRACT, preferred_element_type=F32)
    output = lax.psum_scatter(
        jnp.dot(hidden, gathered, preferred_element_type=F32),
        "tensor",
        scatter_dimension=1,
        tiled=True,
    ).astype(BF)
    d_gate = (d_hidden * up_val * gate_sig * (1.0 + gate_val * (1.0 - gate_sig))).astype(BF)
    d_up = (d_hidden * active).astype(BF)
    grad_cols = lax.all_to_all(full_grad, "dp", split_axis=1, concat_axis=0, tiled=True)
    d_weight = lax.dot_general(
        lax.all_gather(hidden, "dp", axis=0, tiled=True),
        grad_cols,
        ROWS_CONTRACT,
        preferred_element_type=F32,
    )
    d_weight = d_weight * keep_wide.astype(F32)
    return (output, d_gate, d_up, d_weight)


IN_VMEM = pl.BlockSpec(memory_space=pltpu.VMEM)
IN_SMEM = pl.BlockSpec(memory_space=pltpu.SMEM)
ANYWHERE = pl.BlockSpec(memory_space=pl.ANY)


LARGE = 1536 * 1024


def shaped(shape, dtype):
    size = math.prod(shape) * jnp.dtype(dtype).itemsize
    return (pltpu.HBM if size >= LARGE else jax.ShapeDtypeStruct)(shape, dtype)


def placed(a):
    return pltpu.with_memory_space_constraint(a, pltpu.HBM) if a.size * a.dtype.itemsize >= LARGE else a


def ordered(body, deps, operands, out_shape, *, name, pair=None, flops=1, in_specs=None, out_specs=None, grid=(), scratch=(), aliases=None):
    n, m = len(operands), len(deps)
    one = not isinstance(out_shape, (list, tuple))
    operands = [a if a is pair else placed(a) for a in operands]
    deps = [placed(a) for a in deps]

    def run(*refs):
        body(*refs[:n], *refs[n + m :])

    in_specs = [IN_VMEM] * n if in_specs is None else list(in_specs)
    if out_specs is None:
        out_specs = IN_VMEM if one else [IN_VMEM] * len(out_shape)
    return pl.pallas_call(
        run,
        grid=grid,
        in_specs=in_specs + [ANYWHERE] * m,
        out_specs=out_specs,
        out_shape=out_shape,
        scratch_shapes=scratch,
        input_output_aliases=aliases or {},
        compiler_params=pltpu.CompilerParams(vmem_limit_bytes=18 * 2**20),
        cost_estimate=pl.CostEstimate(flops=flops, bytes_accessed=1, transcendentals=0),
        name=name,
    )(*operands, *deps)


def kept(w, mask_ref, row, first, rep):
    n, cols = w.shape[0] // BLK, w.shape[1]
    out = []
    for r in range(n):
        keep = [jnp.full((rep, BLK), mask_ref[row + r, first + k].astype(F32)) for k in range(cols // BLK)]
        m = jnp.concatenate(keep, 1).astype(w.dtype).reshape(1, rep, cols)
        rows = w[r * BLK : (r + 1) * BLK, :].reshape(BLK // rep, rep, cols) * m
        out.append(rows.reshape(BLK, cols))
    return jnp.concatenate(out, 0)


def hidden_of(gate, up, deps):
    rows, hid = gate.shape
    unit = 64

    def body(gate_ref, up_ref, out):
        g = gate_ref[...].astype(F32)
        out[...] = (g * jax.nn.sigmoid(g) * up_ref[...].astype(F32)).astype(BF)

    at = pl.BlockSpec((unit, hid), lambda i: (i, 0))
    return ordered(
        body,
        deps,
        [gate, up],
        shaped((rows, hid), BF),
        grid=(rows // unit,),
        in_specs=[at, at],
        out_specs=at,
        name="hidden",
    )


def masked_pair(info, mask, own, other, deps):
    hid, cols = own.shape
    step = 512

    def body(info_ref, mask_ref, a, b, out):
        row = pl.program_id(0) * (step // BLK)
        x, core = info_ref[0], info_ref[1]
        out[core] = kept(a[...], mask_ref, row, (2 * x + core) * (cols // BLK), 16)
        out[1 - core] = kept(b[...], mask_ref, row, (2 * x + 1 - core) * (cols // BLK), 16)

    w = pl.BlockSpec((step, cols), lambda k: (k, 0))
    pair = ordered(
        body,
        deps,
        [info, mask, own, other],
        pltpu.VMEM((2, hid, cols), BF),
        grid=(hid // step,),
        in_specs=[IN_SMEM, IN_SMEM, w, w],
        out_specs=pl.BlockSpec((2, step, cols), lambda k: (0, k, 0)),
        name="masked_pair",
    )
    return pltpu.with_memory_space_constraint(pair, pltpu.VMEM)


def forward_own(hidden, pair, deps):
    rows, cols = hidden.shape[0], pair.shape[2]

    def body(h, w, out):
        for j in range(2):
            out[j] = jnp.dot(h[...], w[j], preferred_element_type=F32).astype(BF)

    return ordered(body, deps, [hidden, pair], shaped((2, rows, cols), BF), name="forward_own", pair=pair)


def forward_both(info, own, hidden, pair, deps):
    rows, cols = hidden.shape[0], pair.shape[2]

    def body(info_ref, o, h, w, out, passed):
        del passed
        x = info_ref[0]
        for j in range(2):
            part = jnp.dot(h[...], w[j], preferred_element_type=F32).astype(BF)
            out[jnp.where(x == 0, 3 - 2 * j, 2 - 2 * j)] = part
            out[jnp.where(x == 0, 2 * j, 1 + 2 * j)] = o[j]

    return ordered(
        body,
        deps,
        [info, own, hidden, pair],
        [shaped((4, rows, cols), BF), shaped(hidden.shape, BF)],
        in_specs=[IN_SMEM] + [IN_VMEM] * 3,
        out_specs=[IN_VMEM, ANYWHERE],
        aliases={2: 1},
        name="forward_both",
        pair=pair,
    )


def cut(info, grads, deps):
    rows, cols = grads.shape
    half = cols // 2

    def body(info_ref, g, mine, theirs):
        x = info_ref[0]
        mine[...] = g[:, pl.ds(pl.multiple_of(x * half, half), half)]
        theirs[...] = g[:, pl.ds(pl.multiple_of((1 - x) * half, half), half)]

    out = jax.ShapeDtypeStruct((rows, half), BF)
    return ordered(body, deps, [info, grads], [out, out], in_specs=[IN_SMEM, IN_VMEM], name="cut")


def per_core(info, grads, deps):
    rows, cols = grads.shape
    half = cols // 2

    def body(info_ref, g, mine, theirs):
        core = info_ref[1]
        mine[...] = g[:, pl.ds(pl.multiple_of(core * half, half), half)]
        theirs[...] = g[:, pl.ds(pl.multiple_of((1 - core) * half, half), half)]

    out = jax.ShapeDtypeStruct((rows, half), BF)
    return ordered(body, deps, [info, grads], [out, out], in_specs=[IN_SMEM, IN_VMEM], name="per_core")


def back(grads, pair, first, width, dtype, deps, flops=1):
    step = 512
    cols = pair.shape[2]

    def body(g, w, out):
        for k in range(0, width, step):
            rows = slice(first + k, first + k + step)
            part = lax.dot_general(g[:, :cols], w[0, rows, :], COLS_CONTRACT, preferred_element_type=F32)
            part += lax.dot_general(g[:, cols:], w[1, rows, :], COLS_CONTRACT, preferred_element_type=F32)
            out[:, k : k + step] = part.astype(dtype)

    return ordered(body, deps, [grads, pair], shaped((grads.shape[0], width), dtype), name="back", pair=pair, flops=flops)


def relay(a, deps):
    def body(src, out):
        out[...] = src[...]

    return ordered(body, deps, [a], shaped(a.shape, a.dtype), name="relay")


def choose(info, own, received, deps):
    def body(info_ref, a, b, out):
        out[...] = jnp.where(info_ref[2] == 0, a[...], b[...])

    return ordered(
        body, deps, [info, own, received], shaped(own.shape, BF), in_specs=[IN_SMEM, IN_VMEM, IN_VMEM], name="choose"
    )


def hidden_grads(part, part_first, got, gate, up, first, made, deps):
    rows, width = got.shape
    unit = 512

    def body(p, r, gate_ref, up_ref, *refs):
        d_gate, d_up = refs[-2:]
        g, u = gate_ref[...].astype(F32), up_ref[...].astype(F32)
        s = jax.nn.sigmoid(g)
        d_hidden = p[...] + r[...].astype(F32)
        d_gate[...] = (d_hidden * u * s * (1.0 + g * (1.0 - s))).astype(BF)
        d_up[...] = (d_hidden * (g * s)).astype(BF)

    at = pl.BlockSpec((rows, unit), lambda k: (0, first // unit + k))
    part_at = pl.BlockSpec((rows, unit), lambda k: (0, (first - part_first) // unit + k))
    return ordered(
        body,
        deps,
        [part, got, gate, up, *made],
        [shaped(gate.shape, BF)] * 2,
        grid=(width // unit,),
        in_specs=[part_at, pl.BlockSpec((rows, unit), lambda k: (0, k)), at, at] + [ANYWHERE] * len(made),
        out_specs=[at, at],
        aliases={4: 0, 5: 1} if made else None,
        name="hidden_grads",
    )


def weight_grad(info, mask, hidden, grads, deps):
    n = len(hidden)
    rows = sum(h.shape[0] for h in hidden)
    hid, cols = hidden[0].shape[1], grads[0].shape[1]
    step = 512

    def body(info_ref, mask_ref, *refs):
        hid_refs, grad_refs, (out, all_grads) = refs[:n], refs[n:-2], refs[-2:]

        @pl.when(pl.program_id(0) == 0)
        def _():
            at = 0
            for g in grad_refs:
                all_grads[at : at + g.shape[0], :] = g[...]
                at += g.shape[0]

        h = jnp.concatenate([r[...] for r in hid_refs], 0)
        total = lax.dot_general(h, all_grads[...], ROWS_CONTRACT, preferred_element_type=F32)
        row = pl.program_id(0) * (step // BLK)
        out[...] = kept(total, mask_ref, row, (2 * info_ref[0] + info_ref[1]) * (cols // BLK), 8)

    return ordered(
        body,
        deps,
        [info, mask, *hidden, *grads],
        shaped((hid, cols), F32),
        grid=(hid // step,),
        in_specs=[IN_SMEM, IN_SMEM]
        + [pl.BlockSpec((h.shape[0], step), lambda i: (0, i)) for h in hidden]
        + [pl.BlockSpec(g.shape, lambda i: (0, 0)) for g in grads],
        out_specs=pl.BlockSpec((step, cols), lambda i: (i, 0)),
        scratch=[pltpu.VMEM((rows, cols), BF)],
        name="weight_grad",
    )


def four_by_four(gate_pre, up_pre, down_weight, block_mask, grad_out):
    n_t = 4
    d, z = lax.axis_index("dp"), lax.axis_index("tensor")
    x, core = d // 2, d % 2
    q = jnp.where(x == 0, z, n_t - 1 - z)
    tokens, hid = gate_pre.shape
    info = jnp.stack([x, core, q]).astype(jnp.int32)

    def over_x(a):
        return lax.ppermute(a, "dp", [(i, i ^ 2) for i in range(4)])

    def over_core(a):
        return lax.ppermute(a, "dp", [(i, i ^ 1) for i in range(4)])

    def to_owner(a):
        perm = []
        for dd in range(4):
            line = [0, 1, 2, 3] if dd // 2 == 0 else [3, 2, 1, 0]
            perm.append((dd * n_t + line[1], (dd ^ 2) * n_t + line[1]))
            perm.append((dd * n_t + line[2], dd * n_t + line[1]))
            perm.append((dd * n_t + line[3], (dd ^ 2) * n_t + line[0]))
        return lax.ppermute(a, ("dp", "tensor"), perm)

    other = over_core(down_weight)
    full_grad = lax.all_gather(grad_out, "tensor", axis=1, tiled=True)
    h0 = hidden_of(gate_pre, up_pre, [])
    h1 = over_x(h0)
    h2 = over_core(h0)
    pair = masked_pair(info, block_mask, down_weight, other, [h0])
    o0 = forward_own(h0, pair, [h2])
    g0, gx = cut(info, full_grad, [o0])
    g1 = over_x(gx)
    o_all, h1 = forward_both(info, o0, h1, pair, [g0])
    out = lax.psum_scatter(o_all, "tensor", scatter_dimension=0, tiled=False)
    h3 = over_core(h1)
    g0_own, g0_theirs = per_core(info, g0, [o_all])
    parts = [(0, 5 * hid // 8), (5 * hid // 8, hid // 4), (7 * hid // 8, hid // 8)]
    cut_at = parts[1][0]
    own_part = [back(g0, pair, 0, cut_at, F32, [g0_own])]
    last, got = own_part[0], []
    for i, (first, width) in enumerate(parts):
        last = back(g1, pair, first, width, BF, [last], 2 * 10**11 if i == 0 else 1)
        got.append(over_x(last))
    g1_own, g1_theirs = per_core(info, g1, [last])
    own_part.append(back(g0, pair, cut_at, hid - cut_at, F32, [g1_own]))
    g_core = [over_core(g0_theirs), over_core(g1_theirs)]
    d_weight = weight_grad(info, block_mask, [h0, h1, h2, h3], [g0_own, g1_own, *g_core], [own_part[1]])
    made, deps = [], [d_weight]
    for (first, _), g in zip(parts, got):
        own, own_first = (own_part[0], 0) if first < cut_at else (own_part[1], cut_at)
        made, deps = list(hidden_grads(own, own_first, g, gate_pre, up_pre, first, made, deps)), []
    done = relay(out, [d_weight])
    output = choose(info, done, to_owner(done), [made[0]])
    return (output, *made, d_weight)


def solution(mesh):
    fits = mesh.shape["dp"] == 4 and mesh.shape["tensor"] == 4
    return jax.shard_map(
        four_by_four if fits else any_mesh,
        mesh=mesh,
        in_specs=(
            P(("groups", "dp"), "tensor"),
            P(("groups", "dp"), "tensor"),
            P("tensor", "dp"),
            P("tensor", None),
            P(("groups", "dp"), "tensor"),
        ),
        out_specs=(
            P(("groups", "dp"), "tensor"),
            P(("groups", "dp"), "tensor"),
            P(("groups", "dp"), "tensor"),
            P(("groups", "tensor"), "dp"),
        ),
        check_vma=False,
    )
```

```python
import math

import jax
import jax.numpy as jnp
from jax import lax
from jax.experimental import pallas as pl
from jax.experimental.pallas import tpu as pltpu
from jax.sharding import PartitionSpec as P

BLK = 128
BF = jnp.bfloat16
F32 = jnp.float32
ROWS_CONTRACT = (((0,), (0,)), ((), ()))
COLS_CONTRACT = (((1,), (1,)), ((), ()))


def expand_mask(small_mask):
    widened = jnp.repeat(jnp.repeat(small_mask, BLK, axis=0), BLK, axis=1)
    return widened


def any_mesh(gate_pre, up_pre, down_weight, block_mask, grad_out):
    d_local = down_weight.shape[1]
    d_blocks = d_local // BLK
    own_mask = lax.dynamic_slice_in_dim(block_mask, lax.axis_index("dp") * d_blocks, d_blocks, 1)
    keep_wide = expand_mask(own_mask)
    masked = down_weight * keep_wide.astype(BF)
    gate_val = gate_pre.astype(F32)
    up_val = up_pre.astype(F32)
    gate_sig = jax.nn.sigmoid(gate_val)
    active = gate_val * gate_sig
    hidden = (active * up_val).astype(BF)
    full_grad = lax.all_gather(grad_out, "tensor", axis=1, tiled=True)
    gathered = lax.all_gather(masked, "dp", axis=1, tiled=True)
    d_hidden = lax.dot_general(full_grad, gathered, COLS_CONTRACT, preferred_element_type=F32)
    output = lax.psum_scatter(
        jnp.dot(hidden, gathered, preferred_element_type=F32),
        "tensor",
        scatter_dimension=1,
        tiled=True,
    ).astype(BF)
    d_gate = (d_hidden * up_val * gate_sig * (1.0 + gate_val * (1.0 - gate_sig))).astype(BF)
    d_up = (d_hidden * active).astype(BF)
    grad_cols = lax.all_to_all(full_grad, "dp", split_axis=1, concat_axis=0, tiled=True)
    d_weight = lax.dot_general(
        lax.all_gather(hidden, "dp", axis=0, tiled=True),
        grad_cols,
        ROWS_CONTRACT,
        preferred_element_type=F32,
    )
    d_weight = d_weight * keep_wide.astype(F32)
    return (output, d_gate, d_up, d_weight)


IN_VMEM = pl.BlockSpec(memory_space=pltpu.VMEM)
IN_SMEM = pl.BlockSpec(memory_space=pltpu.SMEM)
ANYWHERE = pl.BlockSpec(memory_space=pl.ANY)


LARGE = 1536 * 1024


def shaped(shape, dtype):
    size = math.prod(shape) * jnp.dtype(dtype).itemsize
    return (pltpu.HBM if size >= LARGE else jax.ShapeDtypeStruct)(shape, dtype)


def placed(a):
    return pltpu.with_memory_space_constraint(a, pltpu.HBM) if a.size * a.dtype.itemsize >= LARGE else a


def ordered(body, deps, operands, out_shape, *, name, pair=None, flops=1, in_specs=None, out_specs=None, grid=(), scratch=(), aliases=None):
    n, m = len(operands), len(deps)
    one = not isinstance(out_shape, (list, tuple))
    operands = [a if a is pair else placed(a) for a in operands]
    deps = [placed(a) for a in deps]

    def run(*refs):
        body(*refs[:n], *refs[n + m :])

    in_specs = [IN_VMEM] * n if in_specs is None else list(in_specs)
    if out_specs is None:
        out_specs = IN_VMEM if one else [IN_VMEM] * len(out_shape)
    return pl.pallas_call(
        run,
        grid=grid,
        in_specs=in_specs + [ANYWHERE] * m,
        out_specs=out_specs,
        out_shape=out_shape,
        scratch_shapes=scratch,
        input_output_aliases=aliases or {},
        compiler_params=pltpu.CompilerParams(vmem_limit_bytes=18 * 2**20),
        cost_estimate=pl.CostEstimate(flops=flops, bytes_accessed=1, transcendentals=0),
        name=name,
    )(*operands, *deps)


def kept(w, mask_ref, row, first, rep):
    n, cols = w.shape[0] // BLK, w.shape[1]
    out = []
    for r in range(n):
        keep = [jnp.full((rep, BLK), mask_ref[row + r, first + k].astype(F32)) for k in range(cols // BLK)]
        m = jnp.concatenate(keep, 1).astype(w.dtype).reshape(1, rep, cols)
        rows = w[r * BLK : (r + 1) * BLK, :].reshape(BLK // rep, rep, cols) * m
        out.append(rows.reshape(BLK, cols))
    return jnp.concatenate(out, 0)


def hidden_of(gate, up, deps):
    rows, hid = gate.shape
    unit = 128

    def body(gate_ref, up_ref, out):
        g = gate_ref[...].astype(F32)
        out[...] = (g * jax.nn.sigmoid(g) * up_ref[...].astype(F32)).astype(BF)

    at = pl.BlockSpec((unit, hid), lambda i: (i, 0))
    return ordered(
        body,
        deps,
        [gate, up],
        shaped((rows, hid), BF),
        grid=(rows // unit,),
        in_specs=[at, at],
        out_specs=at,
        name="hidden",
    )


def masked_pair(info, mask, own, other, deps):
    hid, cols = own.shape
    step = 512

    def body(info_ref, mask_ref, a, b, out):
        row = pl.program_id(0) * (step // BLK)
        x, core = info_ref[0], info_ref[1]
        out[core] = kept(a[...], mask_ref, row, (2 * x + core) * (cols // BLK), 16)
        out[1 - core] = kept(b[...], mask_ref, row, (2 * x + 1 - core) * (cols // BLK), 16)

    w = pl.BlockSpec((step, cols), lambda k: (k, 0))
    pair = ordered(
        body,
        deps,
        [info, mask, own, other],
        pltpu.VMEM((2, hid, cols), BF),
        grid=(hid // step,),
        in_specs=[IN_SMEM, IN_SMEM, w, w],
        out_specs=pl.BlockSpec((2, step, cols), lambda k: (0, k, 0)),
        name="masked_pair",
    )
    return pltpu.with_memory_space_constraint(pair, pltpu.VMEM)


def forward_own(hidden, pair, deps):
    rows, cols = hidden.shape[0], pair.shape[2]

    def body(h, w, out):
        for j in range(2):
            out[j] = jnp.dot(h[...], w[j], preferred_element_type=F32).astype(BF)

    return ordered(body, deps, [hidden, pair], shaped((2, rows, cols), BF), name="forward_own", pair=pair)


def forward_both(info, own, hidden, pair, deps):
    rows, cols = hidden.shape[0], pair.shape[2]

    def body(info_ref, o, h, w, out, passed):
        del passed
        x = info_ref[0]
        for j in range(2):
            part = jnp.dot(h[...], w[j], preferred_element_type=F32).astype(BF)
            out[jnp.where(x == 0, 3 - 2 * j, 2 - 2 * j)] = part
            out[jnp.where(x == 0, 2 * j, 1 + 2 * j)] = o[j]

    return ordered(
        body,
        deps,
        [info, own, hidden, pair],
        [shaped((4, rows, cols), BF), shaped(hidden.shape, BF)],
        in_specs=[IN_SMEM] + [IN_VMEM] * 3,
        out_specs=[IN_VMEM, ANYWHERE],
        aliases={2: 1},
        name="forward_both",
        pair=pair,
    )


def cut(info, grads, deps):
    rows, cols = grads.shape
    half = cols // 2

    def body(info_ref, g, mine, theirs):
        x = info_ref[0]
        mine[...] = g[:, pl.ds(pl.multiple_of(x * half, half), half)]
        theirs[...] = g[:, pl.ds(pl.multiple_of((1 - x) * half, half), half)]

    out = jax.ShapeDtypeStruct((rows, half), BF)
    return ordered(body, deps, [info, grads], [out, out], in_specs=[IN_SMEM, IN_VMEM], name="cut")


def per_core(info, grads, deps):
    rows, cols = grads.shape
    half = cols // 2

    def body(info_ref, g, mine, theirs):
        core = info_ref[1]
        mine[...] = g[:, pl.ds(pl.multiple_of(core * half, half), half)]
        theirs[...] = g[:, pl.ds(pl.multiple_of((1 - core) * half, half), half)]

    out = jax.ShapeDtypeStruct((rows, half), BF)
    return ordered(body, deps, [info, grads], [out, out], in_specs=[IN_SMEM, IN_VMEM], name="per_core")


def back(grads, pair, first, width, dtype, deps, flops=1):
    step = 512
    cols = pair.shape[2]

    def body(g, w, out):
        for k in range(0, width, step):
            rows = slice(first + k, first + k + step)
            part = lax.dot_general(g[:, :cols], w[0, rows, :], COLS_CONTRACT, preferred_element_type=F32)
            part += lax.dot_general(g[:, cols:], w[1, rows, :], COLS_CONTRACT, preferred_element_type=F32)
            out[:, k : k + step] = part.astype(dtype)

    return ordered(body, deps, [grads, pair], shaped((grads.shape[0], width), dtype), name="back", pair=pair, flops=flops)


def relay(a, deps):
    def body(src, out):
        out[...] = src[...]

    return ordered(body, deps, [a], shaped(a.shape, a.dtype), name="relay")


def choose(info, own, received, deps):
    def body(info_ref, a, b, out):
        out[...] = jnp.where(info_ref[2] == 0, a[...], b[...])

    return ordered(
        body, deps, [info, own, received], shaped(own.shape, BF), in_specs=[IN_SMEM, IN_VMEM, IN_VMEM], name="choose"
    )


def hidden_grads(part, part_first, got, gate, up, first, made, deps):
    rows, width = got.shape
    unit = 512

    def body(p, r, gate_ref, up_ref, *refs):
        d_gate, d_up = refs[-2:]
        g, u = gate_ref[...].astype(F32), up_ref[...].astype(F32)
        s = jax.nn.sigmoid(g)
        d_hidden = p[...] + r[...].astype(F32)
        d_gate[...] = (d_hidden * u * s * (1.0 + g * (1.0 - s))).astype(BF)
        d_up[...] = (d_hidden * (g * s)).astype(BF)

    at = pl.BlockSpec((rows, unit), lambda k: (0, first // unit + k))
    part_at = pl.BlockSpec((rows, unit), lambda k: (0, (first - part_first) // unit + k))
    return ordered(
        body,
        deps,
        [part, got, gate, up, *made],
        [shaped(gate.shape, BF)] * 2,
        grid=(width // unit,),
        in_specs=[part_at, pl.BlockSpec((rows, unit), lambda k: (0, k)), at, at] + [ANYWHERE] * len(made),
        out_specs=[at, at],
        aliases={4: 0, 5: 1} if made else None,
        name="hidden_grads",
    )


def weight_grad(info, mask, hidden, grads, deps):
    n = len(hidden)
    rows = sum(h.shape[0] for h in hidden)
    hid, cols = hidden[0].shape[1], grads[0].shape[1]
    step = 512

    def body(info_ref, mask_ref, *refs):
        hid_refs, grad_refs, (out, all_grads) = refs[:n], refs[n:-2], refs[-2:]

        @pl.when(pl.program_id(0) == 0)
        def _():
            at = 0
            for g in grad_refs:
                all_grads[at : at + g.shape[0], :] = g[...]
                at += g.shape[0]

        h = jnp.concatenate([r[...] for r in hid_refs], 0)
        total = lax.dot_general(h, all_grads[...], ROWS_CONTRACT, preferred_element_type=F32)
        row = pl.program_id(0) * (step // BLK)
        out[...] = kept(total, mask_ref, row, (2 * info_ref[0] + info_ref[1]) * (cols // BLK), 8)

    return ordered(
        body,
        deps,
        [info, mask, *hidden, *grads],
        shaped((hid, cols), F32),
        grid=(hid // step,),
        in_specs=[IN_SMEM, IN_SMEM]
        + [pl.BlockSpec((h.shape[0], step), lambda i: (0, i)) for h in hidden]
        + [pl.BlockSpec(g.shape, lambda i: (0, 0)) for g in grads],
        out_specs=pl.BlockSpec((step, cols), lambda i: (i, 0)),
        scratch=[pltpu.VMEM((rows, cols), BF)],
        name="weight_grad",
    )


def four_by_four(gate_pre, up_pre, down_weight, block_mask, grad_out):
    n_t = 4
    d, z = lax.axis_index("dp"), lax.axis_index("tensor")
    x, core = d // 2, d % 2
    q = jnp.where(x == 0, z, n_t - 1 - z)
    tokens, hid = gate_pre.shape
    info = jnp.stack([x, core, q]).astype(jnp.int32)

    def over_x(a):
        return lax.ppermute(a, "dp", [(i, i ^ 2) for i in range(4)])

    def over_core(a):
        return lax.ppermute(a, "dp", [(i, i ^ 1) for i in range(4)])

    def to_owner(a):
        perm = []
        for dd in range(4):
            line = [0, 1, 2, 3] if dd // 2 == 0 else [3, 2, 1, 0]
            perm.append((dd * n_t + line[1], (dd ^ 2) * n_t + line[1]))
            perm.append((dd * n_t + line[2], dd * n_t + line[1]))
            perm.append((dd * n_t + line[3], (dd ^ 2) * n_t + line[0]))
        return lax.ppermute(a, ("dp", "tensor"), perm)

    other = over_core(down_weight)
    full_grad = lax.all_gather(grad_out, "tensor", axis=1, tiled=True)
    h0 = hidden_of(gate_pre, up_pre, [])
    h1 = over_x(h0)
    h2 = over_core(h0)
    pair = masked_pair(info, block_mask, down_weight, other, [h0])
    o0 = forward_own(h0, pair, [h2])
    g0, gx = cut(info, full_grad, [o0])
    g1 = over_x(gx)
    o_all, h1 = forward_both(info, o0, h1, pair, [g0])
    out = lax.psum_scatter(o_all, "tensor", scatter_dimension=0, tiled=False)
    h3 = over_core(h1)
    g0_own, g0_theirs = per_core(info, g0, [o_all])
    parts = [(0, 5 * hid // 8), (5 * hid // 8, hid // 4), (7 * hid // 8, hid // 8)]
    cut_at = parts[1][0]
    own_part = [back(g0, pair, 0, cut_at, F32, [g0_own])]
    last, got = own_part[0], []
    for i, (first, width) in enumerate(parts):
        last = back(g1, pair, first, width, BF, [last], 2 * 10**11 if i == 0 else 1)
        got.append(over_x(last))
    g1_own, g1_theirs = per_core(info, g1, [last])
    own_part.append(back(g0, pair, cut_at, hid - cut_at, F32, [g1_own]))
    g_core = [over_core(g0_theirs), over_core(g1_theirs)]
    d_weight = weight_grad(info, block_mask, [h0, h1, h2, h3], [g0_own, g1_own, *g_core], [own_part[1]])
    made, deps = [], [d_weight]
    for (first, _), g in zip(parts, got):
        own, own_first = (own_part[0], 0) if first < cut_at else (own_part[1], cut_at)
        made, deps = list(hidden_grads(own, own_first, g, gate_pre, up_pre, first, made, deps)), []
    done = relay(out, [d_weight])
    output = choose(info, done, to_owner(done), [made[0]])
    return (output, *made, d_weight)


def solution(mesh):
    fits = mesh.shape["dp"] == 4 and mesh.shape["tensor"] == 4
    return jax.shard_map(
        four_by_four if fits else any_mesh,
        mesh=mesh,
        in_specs=(
            P(("groups", "dp"), "tensor"),
            P(("groups", "dp"), "tensor"),
            P("tensor", "dp"),
            P("tensor", None),
            P(("groups", "dp"), "tensor"),
        ),
        out_specs=(
            P(("groups", "dp"), "tensor"),
            P(("groups", "dp"), "tensor"),
            P(("groups", "dp"), "tensor"),
            P(("groups", "tensor"), "dp"),
        ),
        check_vma=False,
    )
```
